32 devices in a mesh: lon: 32 (over z, y, x, core), lat: 1.
Axes of the slice: x: 2, y: 2, z: 4, core: 2. Of those that a mesh axis runs over, the one named last changes fastest.
Arguments:
- fields: bfloat16 [4, 24, 1440, 256], P(None, 'lat', 'lon'), may hold values from -6 to 6
- mix_weight: bfloat16 [256, 256], replicated, may hold values from -0.375 to 0.375
- spectral_weight: float32 [2, 352, 256], P(None, 'lon'), may hold values from -6 to 6
- mode_limit: int32 [24], P('lat'), may hold values from 88 to 352, as said below
- land_mask: int32 [24, 1440], P('lat', 'lon'), may hold values 0 or 1
- forcing: float32 [4, 24, 1440, 128], P(None, 'lat', 'lon'), may hold values from -1440 to 1440
Outputs:
- layer_out: bfloat16 [4, 24, 1440, 256], P(None, 'lat', 'lon')
- residual: float32 [4, 24, 1440, 128], P(None, 'lat', 'lon')
The draws below stay inside these ranges and needn't reach their ends.
Inputs may be any that keep to these rules, and one draw needn't show every extreme that they name: `mode_limit`: some latitude keeps all 352 wavenumbers.
All inputs are finite; a program needn't handle non-finite values. No bound on the sum of `land_mask` on one device may be relied on, other than what follows from the above.
Results may differ from the reference program's by a relative error of at most 0.0055.
Values may be sent and summed in bfloat16 or wider, within the bound.
A program may use at most 64 MiB of HBM per device.

```python
import math
import jax
import jax.numpy as jnp
from jax import lax

C = 256
MODES = 352
MEMBERS = 4
HALF = 128
NLON = 1440
NLAT = 24


def draw_mode_limit(key, part):
    key = jax.random.fold_in(key, 11)
    first_key, second_key = jax.random.split(key)
    values = jax.random.randint(first_key, (NLAT,), MODES // 4, MODES + 1, dtype=jnp.int32)
    chosen = jax.random.randint(second_key, (), 0, NLAT, dtype=jnp.int32)
    places = jnp.arange(NLAT, dtype=jnp.int32)
    return jnp.where(places == chosen, MODES, values).astype(jnp.int32)


def draw_forcing(key, part):
    key = jax.random.fold_in(key, 23)
    shape = (MEMBERS, NLAT, NLON, HALF)
    place = jnp.arange(NLON, dtype=jnp.int32).astype(jnp.float32) / max(NLON - 1, 1)
    values = jnp.clip(jax.random.normal(key, shape, jnp.float32), -4.0, 4.0)
    profile = 0.4 + 1.6 * place
    return (values * profile[None, None, :, None] * (NLON / 8.0)).astype(jnp.float32)


def touch_ends(values, stream_key, smallest, top_value):
    spot = [jax.random.randint(jax.random.fold_in(stream_key, axis), (), 0, length) for axis, length in enumerate(values.shape)]
    widest = values.shape.index(max(values.shape))
    beside = spot[:widest] + [(spot[widest] + 1) % values.shape[widest]] + spot[widest + 1:]
    return values.at[tuple(spot)].set(smallest).at[tuple(beside)].set(top_value)


def steps_of(key, shape, pieces, smallest, largest):
    loudness, own = 1.0, jax.random.fold_in(key, 6)
    for position, blocks in pieces:
        heights = jnp.exp(jax.random.uniform(jax.random.fold_in(own, position), (blocks,), jnp.float32, smallest / len(pieces), largest / len(pieces)))
        loudness = loudness * jnp.repeat(heights, shape[position] // blocks).reshape([-1 if axis == position else 1 for axis in range(len(shape))])
    return loudness


def centred(own_key, extent, scale, limit, shards=(), kind=jnp.bfloat16):
    values = jax.random.normal(own_key, extent, jnp.float32) * scale
    if len(shards) > 0:
        values = steps_of(own_key, extent, shards, -0.22, 0.18) * values
    return jnp.clip(values, min=-limit, max=limit).astype(kind)


def setup_inputs(seed: int = 0) -> dict:
    seeds = jax.random.split(jax.random.key(seed), 7)
    return {
        "fields": centred(seeds[0], (MEMBERS, NLAT, NLON, C), 1.0, 6.0, ((2, 32),)),
        "mix_weight": centred(seeds[1], (C, C), C ** -0.5, 0.375),
        "spectral_weight": centred(seeds[2], (2, MODES, C), 1.0, 6.0, ((1, 32),), jnp.float32),
        "mode_limit": draw_mode_limit(jax.random.fold_in(seeds[6], 71), 0),
        "land_mask": touch_ends((jax.random.randint(seeds[4], (NLAT, NLON), 0, 3) < 2).astype(jnp.int32), jax.random.fold_in(seeds[4], 1), 0, 1),
        "forcing": draw_forcing(jax.random.fold_in(seeds[6], 71), 0),
    }


def build_table(length, wavenumbers):
    order = jnp.arange(wavenumbers, dtype=jnp.int32)[:, None]
    places = jnp.arange(length, dtype=jnp.int32)[None, :]
    angles = (order * places % length).astype(jnp.float32) * (2.0 * math.pi / length)
    return jnp.concatenate([jnp.cos(angles), -jnp.sin(angles)], axis=0).astype(jnp.bfloat16)

def filter_modes(coefficients, weight, limits):
    count = weight.shape[1]
    real_in = coefficients[:, :count]
    imag_in = coefficients[:, count:]
    weight_real = weight[0][None]
    weight_imag = weight[1][None]
    real_out = weight_real * real_in - weight_imag * imag_in
    imag_out = weight_real * imag_in + weight_imag * real_in
    order = jnp.arange(count, dtype=jnp.int32)
    keep_modes = (order[None, :] < limits[:, None]).astype(jnp.float32)
    keep_modes = keep_modes * jnp.where(order == 0, 1.0, 2.0).astype(jnp.float32)[None, :]
    joined = jnp.concatenate([real_out * keep_modes[:, :, None], imag_out * keep_modes[:, :, None]], axis=1)
    return joined.astype(jnp.bfloat16)

def reference(fields, mix_weight, spectral_weight, mode_limit, land_mask, forcing):
    dft_table = build_table(NLON, MODES).astype(jnp.float32)

    def member_term(member):
        coefficients = jnp.einsum('kl,alc->akc', dft_table, member.astype(jnp.float32)) * (1.0 / NLON)
        filtered = filter_modes(coefficients, spectral_weight, mode_limit)
        return jnp.einsum('kl,akc->alc', dft_table, filtered.astype(jnp.float32)).astype(jnp.bfloat16)
    spectral = lax.map(member_term, fields)
    mixed = jnp.dot(fields.reshape(-1, C), mix_weight, preferred_element_type=jnp.float32).reshape(fields.shape)
    summed = lax.optimization_barrier(spectral).astype(jnp.float32) + mixed
    layer_out = (fields.astype(jnp.float32) + jax.nn.gelu(summed)).astype(jnp.bfloat16)
    zonal_flux = layer_out[..., :HALF].astype(jnp.float32)
    merid_flux = layer_out[..., HALF:].astype(jnp.float32)
    zonal = (jnp.roll(zonal_flux, -1, axis=2) - jnp.roll(zonal_flux, 1, axis=2)) * (NLON / (4.0 * math.pi))
    latitude = -0.5 * math.pi + (jnp.arange(NLAT, dtype=jnp.int32).astype(jnp.float32) + 0.5) * (math.pi / NLAT)
    cos_lat = jnp.cos(latitude)
    weighted = merid_flux * cos_lat[None, :, None, None]
    padded = jnp.pad(weighted, ((0, 0), (1, 1), (0, 0), (0, 0)))
    meridional = (padded[:, 2:] - padded[:, :-2]) * (NLAT / (2.0 * math.pi))
    ocean = land_mask.astype(jnp.float32)[None, :, :, None]
    raw = ocean * (zonal + meridional + cos_lat[None, :, None, None] * forcing)
    total = jnp.sum(raw * raw)
    norm = jnp.sqrt(total / (MEMBERS * NLAT * NLON * HALF) + 1e-06)
    return (layer_out, raw / norm)
```

```python
import functools
import math

import jax
import jax.numpy as jnp
import numpy as np
from jax import lax
from jax.experimental import pallas as pl
from jax.experimental.pallas import tpu as pltpu
from jax.sharding import PartitionSpec as P

MESH = pl.DeviceIdType.MESH
PLANE = 8


def tables(length, wavenumbers, count, pad):
    own = length // count
    places = np.arange(count)[:, None] * own + np.arange(pad)[None, :]
    places[:, pad - 1] = np.arange(count) * own - 1
    places = places % length
    order = np.arange(wavenumbers)[:, None, None]
    angles = (order * places[None] % length).astype(np.float32) * np.float32(
        2.0 * math.pi / length
    )
    full = np.concatenate([np.cos(angles), -np.sin(angles)], axis=0)
    inverse = full.reshape(2 * wavenumbers, count * pad).T.astype(jnp.bfloat16)
    full[:, :, own:] = 0.0
    forward = full.reshape(2 * wavenumbers, count * pad)
    return forward.astype(jnp.bfloat16), inverse


def layer_kernel(
    n, lat_dev, own, length, slope, polar, fused,
    fields, mix, weight, limits, table_f, table_i, *rest,
):
    if fused:
        forcing, ocean, cosines, lo, raw, norm = rest[:6]
        rest = rest[6:]
    else:
        lo = rest[0]
        rest = rest[1:]
    (gathered, wr, wi, arrived, filt, outgoing, tf, ti, force, sums,
     fwd_send, fwd_recv, ret_send, ret_recv, gat_send, gat_recv,
     local_sem, sum_send, sum_recv) = rest
    rows, pad, channels = fields.shape
    chunks = rows // n
    per = weight.shape[1]
    modes = per * n
    me = lax.axis_index("lon")
    groups = n // PLANE
    mine = lax.rem(me, PLANE)
    plane = me // PLANE
    stride = n // 3 + 1
    while math.gcd(stride, n) > 1:
        stride += 1

    def send(src, dst, s_sem, r_sem, to):
        return pltpu.make_async_remote_copy(
            src_ref=src, dst_ref=dst, send_sem=s_sem, recv_sem=r_sem,
            device_id={"lon": to}, device_id_type=MESH,
        )

    def await_bytes(ref, sem):
        pltpu.make_async_copy(ref, ref, sem).wait()

    barrier = pltpu.get_barrier_semaphore()

    @pl.loop(1, n)
    def _(i):
        pl.semaphore_signal(
            barrier, inc=1, device_id={"lon": lax.rem(me + i, n)}, device_id_type=MESH
        )

    loads = [
        pltpu.make_async_copy(table_f, tf, local_sem.at[0]),
        pltpu.make_async_copy(table_i, ti, local_sem.at[1]),
    ]
    if fused:
        loads.append(pltpu.make_async_copy(forcing, force, local_sem.at[2]))
    for load in loads:
        load.start()

    slot = mine * groups + plane
    gathered[slot, 0:per] = weight[0]
    gathered[slot, per:2 * per] = weight[1]

    @pl.loop(0, chunks)
    def _(c):
        place = pl.multiple_of(me * pad, 16)
        arrived[c, pl.ds(place, pad)] = fields[c * n + me]

    pl.semaphore_wait(barrier, n - 1)

    @pl.loop(1, groups)
    def _(i):
        to = lax.rem(plane + i, groups) * PLANE + mine
        send(gathered.at[slot], gathered.at[slot], gat_send.at[0], gat_recv.at[0], to).start()

    def scatter(c):
        @pl.loop(1, n)
        def _(i):
            to = lax.rem(me + lax.rem(i * stride, n), n)
            place = pl.multiple_of(me * pad, 16)
            send(
                fields.at[c * n + to], arrived.at[c, pl.ds(place, pad)],
                fwd_send, fwd_recv.at[c], to,
            ).start()

    scatter(0)
    if groups > 1:
        await_bytes(gathered.at[pl.ds(0, groups - 1)], gat_recv.at[0])
    held = gathered.at[pl.ds(mine * groups, groups)]

    @pl.loop(1, PLANE)
    def _(i):
        to = plane * PLANE + lax.rem(mine + i, PLANE)
        send(held, held, gat_send.at[1], gat_recv.at[1], to).start()

    for c in range(1, chunks):
        scatter(c)

    await_bytes(gathered.at[pl.ds(0, n - groups)], gat_recv.at[1])
    for device in range(n):
        place = (device % PLANE) * groups + device // PLANE
        wr[device * per:(device + 1) * per] = gathered[place, 0:per]
        wi[device * per:(device + 1) * per] = gathered[place, per:2 * per]
    loads[0].wait()
    loads[1].wait()

    @pl.loop(0, chunks)
    def _(c):
        await_bytes(arrived.at[c, pl.ds(0, (n - 1) * pad)], fwd_recv.at[c])
        tail = pad - 16
        spot = lax.broadcasted_iota(jnp.int32, (16, channels), 0)

        @pl.loop(0, n)
        def _(d):
            after = pl.multiple_of(lax.rem(d + 1, n) * pad, 16)
            before = pl.multiple_of(lax.rem(d + n - 1, n) * pad + tail, 16)
            here = pl.ds(pl.multiple_of(d * pad + tail, 16), 16)
            first = arrived[c, pl.ds(after, 16)].astype(jnp.float32)
            last = arrived[c, pl.ds(before, 16)].astype(jnp.float32)
            block = arrived[c, here].astype(jnp.float32)
            block = jnp.where(spot == own - tail, pltpu.roll(first, own - tail, 0), block)
            block = jnp.where(spot == 15, pltpu.roll(last, pad - own, 0), block)
            arrived[c, here] = block.astype(jnp.bfloat16)

        whole = arrived[c]
        real = jnp.dot(tf[0:modes], whole, preferred_element_type=jnp.float32) * (1.0 / length)
        imag = jnp.dot(tf[modes:], whole, preferred_element_type=jnp.float32) * (1.0 / length)
        limit = limits[lax.rem(c * n + me, lat_dev)]
        order = lax.broadcasted_iota(jnp.int32, (modes, channels), 0)
        keep = jnp.where(order < limit, jnp.where(order == 0, 1.0, 2.0), 0.0)
        filt[0:modes] = ((wr[...] * real - wi[...] * imag) * keep).astype(jnp.bfloat16)
        filt[modes:] = ((wr[...] * imag + wi[...] * real) * keep).astype(jnp.bfloat16)
        size = PLANE * pad

        @pl.loop(0, groups)
        def _(t):
            target = lax.rem(plane + groups // 2 + t * (groups - 1), groups)
            part = pl.ds(pl.multiple_of(target * size, 16), size)
            here = arrived[c, part]
            spectral = jnp.dot(ti[part], filt[...], preferred_element_type=jnp.float32)
            mixed = jnp.dot(here, mix[...], preferred_element_type=jnp.float32)
            summed = spectral.astype(jnp.bfloat16).astype(jnp.float32) + mixed
            done = here.astype(jnp.float32) + jax.nn.gelu(summed, approximate=True)
            outgoing[pl.ds(c * n + target * PLANE, PLANE)] = done.astype(
                jnp.bfloat16
            ).reshape(PLANE, pad, channels)

            @pl.loop(0, PLANE)
            def _(q):
                to = target * PLANE + lax.rem(mine + q, PLANE)

                @pl.when(to != me)
                def _():
                    send(
                        outgoing.at[c * n + to], lo.at[c * n + me],
                        ret_send, ret_recv.at[c * n + me], to,
                    ).start()

        lo[c * n + me] = outgoing[c * n + me]

    def await_row(r):
        @pl.when(lax.rem(r, n) != me)
        def _():
            await_bytes(lo.at[r], ret_recv.at[r])

    if fused:
        loads[2].wait()
        half = channels // 2
        sums[me] = jnp.zeros((8, half), jnp.float32)

        def residual(r):
            j = lax.rem(r, lat_dev)
            zonal = lo[r, :, 0:half].astype(jnp.float32)
            zonal = (pltpu.roll(zonal, pad - 1, 0) - pltpu.roll(zonal, 1, 0)) * slope
            north = lo[jnp.minimum(r + 1, rows - 1), :, half:].astype(jnp.float32)
            south = lo[jnp.maximum(r - 1, 0), :, half:].astype(jnp.float32)
            merid = (north * cosines[j + 2] - south * cosines[j]) * polar
            flow = (zonal + merid)[0:own]
            value = ocean[j] * (flow + cosines[j + 1] * force[r])
            raw[r] = value
            sums[me, 0:1] += jnp.sum(value * value, axis=0, keepdims=True)

        await_row(0)

        @pl.loop(1, rows)
        def _(r):
            await_row(r)
            residual(r - 1)

        residual(rows - 1)

        @pl.loop(1, n)
        def _(i):
            to = lax.rem(me + i, n)
            send(sums.at[me], sums.at[me], sum_send, sum_recv, to).start()

        await_bytes(sums.at[pl.ds(0, n - 1)], sum_recv)
        total = jnp.sum(sums[...], axis=0)
        total = jnp.sum(jnp.sum(total, axis=0, keepdims=True), axis=1, keepdims=True)
        scale = 1.0 / (rows * own * n * half)
        norm[...] = jnp.broadcast_to(jnp.sqrt(total * scale + 1e-06), (8, half))
        await_bytes(sums.at[pl.ds(0, n - 1)], sum_send)
    else:
        @pl.loop(0, rows)
        def _(r):
            await_row(r)

    await_bytes(fields.at[pl.ds(0, chunks * (n - 1))], fwd_send)
    await_bytes(outgoing.at[pl.ds(0, chunks * (n - 1))], ret_send)
    if groups > 1:
        await_bytes(gathered.at[pl.ds(0, groups - 1)], gat_send.at[0])
    await_bytes(gathered.at[pl.ds(0, (PLANE - 1) * groups)], gat_send.at[1])


def extended(block, axis, dim):
    count = lax.axis_size(axis)
    forward = [(i, i + 1) for i in range(count - 1)]
    if axis == "lon":
        forward.append((count - 1, 0))
    backward = [(target, source) for source, target in forward]
    low = lax.ppermute(lax.slice_in_dim(block, block.shape[dim] - 1, None, axis=dim), axis, forward)
    high = lax.ppermute(lax.slice_in_dim(block, 0, 1, axis=dim), axis, backward)
    return jnp.concatenate([low, block, high], axis=dim)


def per_device(fields, mix_weight, spectral_weight, mode_limit, land_mask, forcing):
    members, lat_dev, own, channels = fields.shape
    half = channels // 2
    n = lax.axis_size("lon")
    lat_count = lax.axis_size("lat")
    length = own * n
    nlat = lat_dev * lat_count
    rows = members * lat_dev
    chunks = rows // n
    per = spectral_weight.shape[1]
    modes = per * n
    pad = -(-(own + 2) // 16) * 16
    fused = lat_count == 1
    forward, inverse = tables(length, modes, n, pad)
    slope = length / (4.0 * math.pi)
    polar = nlat / (2.0 * math.pi)
    padded = jnp.pad(fields.reshape(rows, own, channels), ((0, 0), (0, pad - own), (0, 0)))
    vmem = pl.BlockSpec(memory_space=pltpu.VMEM)
    smem = pl.BlockSpec(memory_space=pltpu.SMEM)
    away = pl.BlockSpec(memory_space=pl.ANY)
    operands = [padded, mix_weight, spectral_weight, mode_limit,
                jnp.asarray(forward), jnp.asarray(inverse)]
    in_specs = [vmem, vmem, vmem, smem, away, away]
    out_shape = [jax.ShapeDtypeStruct((rows, pad, channels), jnp.bfloat16)]
    if fused:
        latitude = np.float32(-0.5 * math.pi) + (
            np.arange(nlat, dtype=np.float32) + np.float32(0.5)
        ) * np.float32(math.pi / nlat)
        cosines = np.zeros((nlat + 2,), np.float32)
        cosines[1:-1] = np.cos(latitude)
        ocean = jnp.broadcast_to(
            land_mask.astype(jnp.float32)[:, :, None], (lat_dev, own, half)
        )
        operands += [forcing.reshape(rows, own, half), ocean, jnp.asarray(cosines)]
        in_specs += [away, vmem, smem]
        out_shape += [
            jax.ShapeDtypeStruct((rows, own, half), jnp.float32),
            jax.ShapeDtypeStruct((8, half), jnp.float32),
        ]
    gat_rows = -(-2 * per // 8) * 8
    dma = pltpu.SemaphoreType.DMA
    results = pl.pallas_call(
        functools.partial(
            layer_kernel, n, lat_dev, own, length, slope, polar, fused
        ),
        out_shape=out_shape,
        in_specs=in_specs,
        out_specs=[vmem] * len(out_shape),
        scratch_shapes=[
            pltpu.VMEM((n, gat_rows, channels), jnp.float32),
            pltpu.VMEM((modes, channels), jnp.float32),
            pltpu.VMEM((modes, channels), jnp.float32),
            pltpu.VMEM((chunks, n * pad, channels), jnp.bfloat16),
            pltpu.VMEM((2 * modes, channels), jnp.bfloat16),
            pltpu.VMEM((rows, pad, channels), jnp.bfloat16),
            pltpu.VMEM(forward.shape, jnp.bfloat16),
            pltpu.VMEM(inverse.shape, jnp.bfloat16),
            pltpu.VMEM((rows, own, half) if fused else (8, half), jnp.float32),
            pltpu.VMEM((n, 8, half), jnp.float32),
            dma, dma((chunks,)), dma, dma((rows,)), dma((2,)), dma((2,)),
            dma((3,)), dma, dma,
        ],
        compiler_params=pltpu.CompilerParams(
            collective_id=0, has_side_effects=True, vmem_limit_bytes=48 * 2**20
        ),
    )(*operands)
    layer_out = results[0][:, :own].reshape(fields.shape)
    if fused:
        residual = results[1].reshape(forcing.shape) / results[2][0]
        return layer_out, residual
    zonal = extended(layer_out[..., :half], "lon", 2).astype(jnp.float32)
    zonal = (zonal[:, :, 2:] - zonal[:, :, :-2]) * slope
    merid = extended(layer_out[..., half:], "lat", 1).astype(jnp.float32)
    lat_ids = lax.axis_index("lat") * lat_dev + jnp.arange(-1, lat_dev + 1, dtype=jnp.int32)
    latitude = -0.5 * math.pi + (lat_ids.astype(jnp.float32) + 0.5) * (math.pi / nlat)
    cos_lat = jnp.cos(latitude)
    weighted = merid * cos_lat[None, :, None, None]
    merid = (weighted[:, 2:] - weighted[:, :-2]) * polar
    ocean = land_mask.astype(jnp.float32)[None, :, :, None]
    raw = ocean * (zonal + merid + cos_lat[1:-1][None, :, None, None] * forcing)
    total = lax.psum(jnp.sum(raw * raw), ("lon", "lat"))
    norm = jnp.sqrt(total / (members * nlat * length * half) + 1e-06)
    return layer_out, raw / norm


def solution(mesh):
    placed = (
        P(None, "lat", "lon", None),
        P(),
        P(None, "lon", None),
        P("lat"),
        P("lat", "lon"),
        P(None, "lat", "lon", None),
    )
    return jax.shard_map(
        per_device,
        mesh=mesh,
        in_specs=placed,
        out_specs=(P(None, "lat", "lon", None), P(None, "lat", "lon", None)),
        check_vma=False,
    )
```

```python
import functools
import math

import jax
import jax.numpy as jnp
import numpy as np
from jax import lax
from jax.experimental import pallas as pl
from jax.experimental.pallas import tpu as pltpu
from jax.sharding import PartitionSpec as P

MESH = pl.DeviceIdType.MESH
PLANE = 8


def tables(length, wavenumbers, count, pad):
    own = length // count
    places = np.arange(count)[:, None] * own + np.arange(pad)[None, :]
    places[:, pad - 1] = np.arange(count) * own - 1
    places = places % length
    order = np.arange(wavenumbers)[:, None, None]
    angles = (order * places[None] % length).astype(np.float32) * np.float32(
        2.0 * math.pi / length
    )
    full = np.concatenate([np.cos(angles), -np.sin(angles)], axis=0)
    inverse = full.reshape(2 * wavenumbers, count * pad).T.astype(jnp.bfloat16)
    full[:, :, own:] = 0.0
    forward = full.reshape(2 * wavenumbers, count * pad)
    return forward.astype(jnp.bfloat16), inverse


def layer_kernel(
    n, lat_dev, own, length, slope, polar, fused,
    native, mix, weight, limits, table_f, table_i, *rest,
):
    if fused:
        forcing, ocean, cosines, lo_rows, raw, norm = rest[:6]
        rest = rest[6:]
    else:
        lo_rows = rest[0]
        rest = rest[1:]
    (fields, staged, lo, gathered, wr, wi, arrived, filt, outgoing, tf, ti,
     force, sums, squares,
     fwd_send, fwd_recv, ret_send, ret_recv, gat_send, gat_recv,
     local_sem, sum_send, sum_recv) = rest
    rows, pad, channels = fields.shape
    chunks = rows // n
    members = rows // lat_dev
    cells = own * lat_dev
    per = weight.shape[0]
    modes = per * n
    me = lax.axis_index("lon")
    groups = n // PLANE
    mine = lax.rem(me, PLANE)
    plane = me // PLANE
    stride = n // 3 + 1
    while math.gcd(stride, n) > 1:
        stride += 1

    def send(src, dst, s_sem, r_sem, to):
        return pltpu.make_async_remote_copy(
            src_ref=src, dst_ref=dst, send_sem=s_sem, recv_sem=r_sem,
            device_id={"lon": to}, device_id_type=MESH,
        )

    def await_bytes(ref, sem):
        pltpu.make_async_copy(ref, ref, sem).wait()

    barrier = pltpu.get_barrier_semaphore()

    @pl.loop(1, n)
    def _(i):
        pl.semaphore_signal(
            barrier, inc=1, device_id={"lon": lax.rem(me + i, n)}, device_id_type=MESH
        )

    loads = [
        pltpu.make_async_copy(table_f, tf, local_sem.at[0]),
        pltpu.make_async_copy(table_i, ti, local_sem.at[1]),
    ]
    if fused:
        loads.append(pltpu.make_async_copy(forcing, force, local_sem.at[2]))
    for load in loads:
        load.start()

    slot = mine * groups + plane
    gathered[slot, 0:per] = weight[:, 0]
    gathered[slot, per:2 * per] = weight[:, 1]
    lanes = [slice(part, part + 128) for part in range(0, channels, 128)]
    for s in range(len(lanes)):
        staged[s, cells:] = jnp.zeros(((pad - own) * lat_dev, 128), jnp.float32)

    def prepare(m):
        start = m * cells
        for s, part in enumerate(lanes):
            staged[s, 0:cells] = native[start:start + cells, part].astype(jnp.float32)

        @pl.loop(0, lat_dev)
        def _(j):
            for s, part in enumerate(lanes):
                row = staged[s, pl.ds(j, pad, stride=lat_dev), :]
                fields[m * lat_dev + j, :, part] = row.astype(jnp.bfloat16)

    ready = 0
    while ready < members and ready * lat_dev < n:
        prepare(ready)
        ready += 1
    pl.semaphore_wait(barrier, n - 1)

    @pl.loop(1, groups)
    def _(i):
        to = lax.rem(plane + i, groups) * PLANE + mine
        send(gathered.at[slot], gathered.at[slot], gat_send.at[0], gat_recv.at[0], to).start()

    def scatter(c):
        @pl.loop(1, n)
        def _(i):
            to = lax.rem(me + lax.rem(i * stride, n), n)
            place = pl.multiple_of(me * pad, 16)
            send(
                fields.at[c * n + to], arrived.at[c, pl.ds(place, pad)],
                fwd_send, fwd_recv.at[c], to,
            ).start()

        place = pl.multiple_of(me * pad, 16)
        arrived[c, pl.ds(place, pad)] = fields[c * n + me]

    scatter(0)
    if groups > 1:
        await_bytes(gathered.at[pl.ds(0, groups - 1)], gat_recv.at[0])
    held = gathered.at[pl.ds(mine * groups, groups)]

    @pl.loop(1, PLANE)
    def _(i):
        to = plane * PLANE + lax.rem(mine + i, PLANE)
        send(held, held, gat_send.at[1], gat_recv.at[1], to).start()

    for c in range(1, chunks):
        while ready < members and ready * lat_dev < (c + 1) * n:
            prepare(ready)
            ready += 1
        scatter(c)

    await_bytes(gathered.at[pl.ds(0, n - groups)], gat_recv.at[1])
    for device in range(n):
        place = (device % PLANE) * groups + device // PLANE
        wr[device * per:(device + 1) * per] = gathered[place, 0:per]
        wi[device * per:(device + 1) * per] = gathered[place, per:2 * per]
    loads[0].wait()
    loads[1].wait()

    @pl.loop(0, chunks)
    def _(c):
        await_bytes(arrived.at[c, pl.ds(0, (n - 1) * pad)], fwd_recv.at[c])
        tail = pad - 16
        spot = lax.broadcasted_iota(jnp.int32, (16, channels), 0)

        @pl.loop(0, n)
        def _(d):
            after = pl.multiple_of(lax.rem(d + 1, n) * pad, 16)
            before = pl.multiple_of(lax.rem(d + n - 1, n) * pad + tail, 16)
            here = pl.ds(pl.multiple_of(d * pad + tail, 16), 16)
            first = arrived[c, pl.ds(after, 16)].astype(jnp.float32)
            last = arrived[c, pl.ds(before, 16)].astype(jnp.float32)
            block = arrived[c, here].astype(jnp.float32)
            block = jnp.where(spot == own - tail, pltpu.roll(first, own - tail, 0), block)
            block = jnp.where(spot == 15, pltpu.roll(last, pad - own, 0), block)
            arrived[c, here] = block.astype(jnp.bfloat16)

        whole = arrived[c]
        real = jnp.dot(tf[0:modes], whole, preferred_element_type=jnp.float32) * (1.0 / length)
        imag = jnp.dot(tf[modes:], whole, preferred_element_type=jnp.float32) * (1.0 / length)
        limit = limits[lax.rem(c * n + me, lat_dev)]
        order = lax.broadcasted_iota(jnp.int32, (modes, channels), 0)
        keep = jnp.where(order < limit, jnp.where(order == 0, 1.0, 2.0), 0.0)
        filt[0:modes] = ((wr[...] * real - wi[...] * imag) * keep).astype(jnp.bfloat16)
        filt[modes:] = ((wr[...] * imag + wi[...] * real) * keep).astype(jnp.bfloat16)
        size = PLANE * pad

        @pl.loop(0, groups)
        def _(t):
            target = lax.rem(plane + groups // 2 + t * (groups - 1), groups)
            part = pl.ds(pl.multiple_of(target * size, 16), size)
            here = arrived[c, part]
            spectral = jnp.dot(ti[part], filt[...], preferred_element_type=jnp.float32)
            mixed = jnp.dot(here, mix[...], preferred_element_type=jnp.float32)
            summed = spectral.astype(jnp.bfloat16).astype(jnp.float32) + mixed
            done = here.astype(jnp.float32) + jax.nn.gelu(summed, approximate=True)
            outgoing[pl.ds(c * n + target * PLANE, PLANE)] = done.astype(
                jnp.bfloat16
            ).reshape(PLANE, pad, channels)

            @pl.loop(0, PLANE)
            def _(q):
                to = target * PLANE + lax.rem(mine + q, PLANE)

                @pl.when(to != me)
                def _():
                    send(
                        outgoing.at[c * n + to], lo.at[c * n + me],
                        ret_send, ret_recv.at[c * n + me], to,
                    ).start()

        lo[c * n + me] = outgoing[c * n + me]

    def await_row(r):
        @pl.when(lax.rem(r, n) != me)
        def _():
            await_bytes(lo.at[r], ret_recv.at[r])

    half = channels // 2

    def keep_row(r, j):
        for s, part in enumerate(lanes):
            row = lo[r, :, part].astype(jnp.float32)[0:own]
            staged[s, pl.ds(j, own, stride=lat_dev), :] = row

    def keep_member(m):
        start = pl.multiple_of(m * cells, 8)
        for s, part in enumerate(lanes):
            lo_rows[pl.ds(start, cells), part] = staged[s, 0:cells].astype(jnp.bfloat16)

    if fused:
        loads[2].wait()
        squares[...] = jnp.zeros_like(squares)

        def residual(m, j):
            r = m * lat_dev + j
            zonal = lo[r, :, 0:half].astype(jnp.float32)
            zonal = (pltpu.roll(zonal, pad - 1, 0) - pltpu.roll(zonal, 1, 0)) * slope
            north = lo[m * lat_dev + jnp.minimum(j + 1, lat_dev - 1), :, half:].astype(jnp.float32)
            south = lo[m * lat_dev + jnp.maximum(j - 1, 0), :, half:].astype(jnp.float32)
            merid = (north * cosines[j + 2] - south * cosines[j]) * polar
            flow = (zonal + merid)[0:own]
            spread = pl.ds(m * cells + j, own, stride=lat_dev)
            value = flow + cosines[j + 1] * force[spread, :]
            value = ocean[j].astype(jnp.float32) * value
            raw[spread, :] = value
            return value * value

        step = 2 if lat_dev % 2 == 0 else 1

        @pl.loop(0, members)
        def _(m):
            await_row(m * lat_dev)

            @pl.loop(0, lat_dev, step=step)
            def _(j):
                for k in range(1, step):
                    await_row(m * lat_dev + j + k)

                @pl.when(j + step < lat_dev)
                def _():
                    await_row(m * lat_dev + j + step)

                total = residual(m, j)
                keep_row(m * lat_dev + j, j)
                for k in range(1, step):
                    total += residual(m, j + k)
                    keep_row(m * lat_dev + j + k, j + k)
                squares[...] += total

            keep_member(m)

        sums[me] = jnp.broadcast_to(
            jnp.sum(squares[...], axis=0, keepdims=True) * 0.125, (8, half)
        )

        @pl.loop(1, n)
        def _(i):
            to = lax.rem(me + i, n)
            send(sums.at[me], sums.at[me], sum_send, sum_recv, to).start()

        await_bytes(sums.at[pl.ds(0, n - 1)], sum_recv)
        total = jnp.sum(sums[...], axis=0)
        total = jnp.sum(jnp.sum(total, axis=0, keepdims=True), axis=1, keepdims=True)
        scale = 1.0 / (rows * own * n * half)
        norm[...] = jnp.broadcast_to(jnp.sqrt(total * scale + 1e-06), (8, half))
        await_bytes(sums.at[pl.ds(0, n - 1)], sum_send)
    else:
        @pl.loop(0, members)
        def _(m):
            @pl.loop(0, lat_dev)
            def _(j):
                await_row(m * lat_dev + j)
                keep_row(m * lat_dev + j, j)

            keep_member(m)

    await_bytes(fields.at[pl.ds(0, chunks * (n - 1))], fwd_send)
    await_bytes(outgoing.at[pl.ds(0, chunks * (n - 1))], ret_send)
    if groups > 1:
        await_bytes(gathered.at[pl.ds(0, groups - 1)], gat_send.at[0])
    await_bytes(gathered.at[pl.ds(0, (PLANE - 1) * groups)], gat_send.at[1])


def extended(block, axis, dim):
    count = lax.axis_size(axis)
    forward = [(i, i + 1) for i in range(count - 1)]
    if axis == "lon":
        forward.append((count - 1, 0))
    backward = [(target, source) for source, target in forward]
    low = lax.ppermute(lax.slice_in_dim(block, block.shape[dim] - 1, None, axis=dim), axis, forward)
    high = lax.ppermute(lax.slice_in_dim(block, 0, 1, axis=dim), axis, backward)
    return jnp.concatenate([low, block, high], axis=dim)


def per_device(fields, mix_weight, spectral_weight, mode_limit, land_mask, forcing):
    members, lat_dev, own, channels = fields.shape
    half = channels // 2
    n = lax.axis_size("lon")
    lat_count = lax.axis_size("lat")
    length = own * n
    nlat = lat_dev * lat_count
    rows = members * lat_dev
    chunks = rows // n
    per = spectral_weight.shape[1]
    modes = per * n
    pad = -(-(own + 2) // 16) * 16
    fused = lat_count == 1
    forward, inverse = tables(length, modes, n, pad)
    slope = length / (4.0 * math.pi)
    polar = nlat / (2.0 * math.pi)
    cells = own * lat_dev

    def by_longitude(array):
        return array.transpose(0, 2, 1, 3).reshape(members * cells, array.shape[3])

    def by_latitude(array):
        shape = (members, own, lat_dev, array.shape[1])
        return array.reshape(shape).transpose(0, 2, 1, 3)

    vmem = pl.BlockSpec(memory_space=pltpu.VMEM)
    smem = pl.BlockSpec(memory_space=pltpu.SMEM)
    away = pl.BlockSpec(memory_space=pl.ANY)
    operands = [by_longitude(fields), mix_weight, spectral_weight.transpose(1, 0, 2), mode_limit,
                jnp.asarray(forward), jnp.asarray(inverse)]
    in_specs = [vmem, vmem, vmem, smem, away, away]
    out_shape = [jax.ShapeDtypeStruct((members * cells, channels), jnp.bfloat16)]
    if fused:
        latitude = np.float32(-0.5 * math.pi) + (
            np.arange(nlat, dtype=np.float32) + np.float32(0.5)
        ) * np.float32(math.pi / nlat)
        cosines = np.zeros((nlat + 2,), np.float32)
        cosines[1:-1] = np.cos(latitude)
        ocean = jnp.broadcast_to(land_mask[:, :, None], (lat_dev, own, half))
        operands += [by_longitude(forcing), ocean, jnp.asarray(cosines)]
        in_specs += [away, vmem, smem]
        out_shape += [
            jax.ShapeDtypeStruct((members * cells, half), jnp.float32),
            jax.ShapeDtypeStruct((8, half), jnp.float32),
        ]
    gat_rows = -(-2 * per // 8) * 8
    dma = pltpu.SemaphoreType.DMA
    results = pl.pallas_call(
        functools.partial(
            layer_kernel, n, lat_dev, own, length, slope, polar, fused
        ),
        out_shape=out_shape,
        in_specs=in_specs,
        out_specs=[vmem] * len(out_shape),
        scratch_shapes=[
            pltpu.VMEM((rows, pad, channels), jnp.bfloat16),
            pltpu.VMEM((channels // 128, pad * lat_dev, 128), jnp.float32),
            pltpu.VMEM((rows, pad, channels), jnp.bfloat16),
            pltpu.VMEM((n, gat_rows, channels), jnp.float32),
            pltpu.VMEM((modes, channels), jnp.float32),
            pltpu.VMEM((modes, channels), jnp.float32),
            pltpu.VMEM((chunks, n * pad, channels), jnp.bfloat16),
            pltpu.VMEM((2 * modes, channels), jnp.bfloat16),
            pltpu.VMEM((rows, pad, channels), jnp.bfloat16),
            pltpu.VMEM(forward.shape, jnp.bfloat16),
            pltpu.VMEM(inverse.shape, jnp.bfloat16),
            pltpu.VMEM((members * cells, half) if fused else (8, half), jnp.float32),
            pltpu.VMEM((n, 8, half), jnp.float32),
            pltpu.VMEM((own, half), jnp.float32),
            dma, dma((chunks,)), dma, dma((rows,)), dma((2,)), dma((2,)),
            dma((3,)), dma, dma,
        ],
        compiler_params=pltpu.CompilerParams(
            collective_id=0, has_side_effects=True, vmem_limit_bytes=48 * 2**20
        ),
    )(*operands)
    layer_out = by_latitude(results[0])
    if fused:
        residual = by_latitude(results[1] / results[2][0:1])
        return layer_out, residual
    zonal = extended(layer_out[..., :half], "lon", 2).astype(jnp.float32)
    zonal = (zonal[:, :, 2:] - zonal[:, :, :-2]) * slope
    merid = extended(layer_out[..., half:], "lat", 1).astype(jnp.float32)
    lat_ids = lax.axis_index("lat") * lat_dev + jnp.arange(-1, lat_dev + 1, dtype=jnp.int32)
    latitude = -0.5 * math.pi + (lat_ids.astype(jnp.float32) + 0.5) * (math.pi / nlat)
    cos_lat = jnp.cos(latitude)
    weighted = merid * cos_lat[None, :, None, None]
    merid = (weighted[:, 2:] - weighted[:, :-2]) * polar
    ocean = land_mask.astype(jnp.float32)[None, :, :, None]
    raw = ocean * (zonal + merid + cos_lat[1:-1][None, :, None, None] * forcing)
    total = lax.psum(jnp.sum(raw * raw), ("lon", "lat"))
    norm = jnp.sqrt(total / (members * nlat * length * half) + 1e-06)
    return layer_out, raw / norm


def solution(mesh):
    placed = (
        P(None, "lat", "lon", None),
        P(),
        P(None, "lon", None),
        P("lat"),
        P("lat", "lon"),
        P(None, "lat", "lon", None),
    )
    return jax.shard_map(
        per_device,
        mesh=mesh,
        in_specs=placed,
        out_specs=(P(None, "lat", "lon", None), P(None, "lat", "lon", None)),
        check_vma=False,
    )
```

```python
import functools
import math

import jax
import jax.numpy as jnp
import numpy as np
from jax import lax
from jax.experimental import pallas as pl
from jax.experimental.pallas import tpu as pltpu
from jax.sharding import PartitionSpec as P

MESH = pl.DeviceIdType.MESH
PLANE = 8


def tables(length, wavenumbers, count, pad):
    own = length // count
    places = np.arange(count)[:, None] * own + np.arange(pad)[None, :]
    places[:, pad - 1] = np.arange(count) * own - 1
    places = places % length
    order = np.arange(wavenumbers)[:, None, None]
    angles = (order * places[None] % length).astype(np.float32) * np.float32(
        2.0 * math.pi / length
    )
    full = np.concatenate([np.cos(angles), -np.sin(angles)], axis=0)
    inverse = full.reshape(2 * wavenumbers, count * pad).T.astype(jnp.bfloat16)
    full[:, :, own:] = 0.0
    forward = full.reshape(2 * wavenumbers, count * pad)
    return forward.astype(jnp.bfloat16), inverse


def layer_kernel(
    n, lat_dev, own, length, slope, polar, fused,
    fields_in, mix_in, weight_in, limits_in, table_f, table_i, *rest,
):
    if fused:
        forcing, mask_in, cos_in, lo_rows, raw = rest[:5]
        rest = rest[5:]
    else:
        lo_rows = rest[0]
        rest = rest[1:]
    (native, mix, weight, limits, mask, cosines, ocean, fields, staged, lo, gathered, wr, wi, arrived, filt, outgoing, tf, ti,
     force, sums, squares,
     fwd_send, fwd_recv, ret_send, ret_recv, gat_send, gat_recv,
     local_sem, sum_send, sum_recv) = rest
    rows, pad, channels = fields.shape
    chunks = rows // n
    members = rows // lat_dev
    cells = own * lat_dev
    per = weight.shape[0]
    modes = per * n
    me = lax.axis_index("lon")
    groups = n // PLANE
    mine = lax.rem(me, PLANE)
    plane = me // PLANE
    stride = n // 3 + 1
    while math.gcd(stride, n) > 1:
        stride += 1

    def send(src, dst, s_sem, r_sem, to):
        return pltpu.make_async_remote_copy(
            src_ref=src, dst_ref=dst, send_sem=s_sem, recv_sem=r_sem,
            device_id={"lon": to}, device_id_type=MESH,
        )

    def await_bytes(ref, sem):
        pltpu.make_async_copy(ref, ref, sem).wait()

    barrier = pltpu.get_barrier_semaphore()

    @pl.loop(1, n)
    def _(i):
        pl.semaphore_signal(
            barrier, inc=1, device_id={"lon": lax.rem(me + i, n)}, device_id_type=MESH
        )

    pairs = [(weight_in, weight)]
    for m in range(members):
        pairs.append((fields_in.at[m], native.at[m]))
    pairs += [(table_f, tf), (table_i, ti), (mix_in, mix), (limits_in, limits)]
    if fused:
        pairs += [(mask_in, mask), (cos_in, cosines), (forcing, force)]
    loads = [
        pltpu.make_async_copy(src, dst, local_sem.at[i]) for i, (src, dst) in enumerate(pairs)
    ]
    for load in loads:
        load.start()
    loads[0].wait()

    slot = mine * groups + plane
    gathered[slot, 0:per] = weight[:, 0]
    gathered[slot, per:2 * per] = weight[:, 1]
    lanes = [slice(part, part + 128) for part in range(0, channels, 128)]
    for s in range(len(lanes)):
        staged[s, cells:] = jnp.zeros(((pad - own) * lat_dev, 128), jnp.float32)

    def prepare(m):
        loads[1 + m].wait()
        for s, part in enumerate(lanes):
            staged[s, 0:cells] = native[m, :, part].astype(jnp.float32)

        @pl.loop(0, lat_dev)
        def _(j):
            for s, part in enumerate(lanes):
                row = staged[s, pl.ds(j, pad, stride=lat_dev), :]
                fields[m * lat_dev + j, :, part] = row.astype(jnp.bfloat16)

    ready = 0
    while ready < members and ready * lat_dev < n:
        prepare(ready)
        ready += 1
    pl.semaphore_wait(barrier, n - 1)

    @pl.loop(1, groups)
    def _(i):
        to = lax.rem(plane + i, groups) * PLANE + mine
        send(gathered.at[slot], gathered.at[slot], gat_send.at[0], gat_recv.at[0], to).start()

    def scatter(c):
        @pl.loop(1, n)
        def _(i):
            to = lax.rem(me + lax.rem(i * stride, n), n)
            place = pl.multiple_of(me * pad, 16)
            send(
                fields.at[c * n + to], arrived.at[c, pl.ds(place, pad)],
                fwd_send.at[c], fwd_recv.at[c], to,
            ).start()

        place = pl.multiple_of(me * pad, 16)
        arrived[c, pl.ds(place, pad)] = fields[c * n + me]

    scatter(0)
    if groups > 1:
        await_bytes(gathered.at[pl.ds(0, groups - 1)], gat_recv.at[0])
    held = gathered.at[pl.ds(mine * groups, groups)]

    @pl.loop(1, PLANE)
    def _(i):
        to = plane * PLANE + lax.rem(mine + i, PLANE)
        send(held, held, gat_send.at[1], gat_recv.at[1], to).start()

    for c in range(1, chunks):
        while ready < members and ready * lat_dev < (c + 1) * n:
            prepare(ready)
            ready += 1
        if c >= 2:
            await_bytes(fields.at[pl.ds(0, n - 1)], fwd_send.at[c - 2])
        scatter(c)

    for load in loads[1 + members:]:
        load.wait()
    if fused:
        eye = [lax.broadcasted_iota(jnp.int32, (own, own), k) for k in range(2)]
        eye = (eye[0] == eye[1]).astype(jnp.bfloat16)
        turned = lax.dot_general(
            eye, mask[...].astype(jnp.float32).astype(jnp.bfloat16), (((1,), (1,)), ((), ())),
            preferred_element_type=jnp.float32,
        ).astype(jnp.bfloat16)
        row_of = lax.broadcasted_iota(jnp.int32, (lat_dev, channels // 2), 0)

        @pl.loop(0, lat_dev)
        def _(j):
            chosen = (row_of == j).astype(jnp.float32).astype(jnp.bfloat16)
            ocean[j] = jnp.dot(turned, chosen, preferred_element_type=jnp.float32)

    await_bytes(gathered.at[pl.ds(0, n - groups)], gat_recv.at[1])
    for device in range(n):
        place = (device % PLANE) * groups + device // PLANE
        wr[device * per:(device + 1) * per] = gathered[place, 0:per]
        wi[device * per:(device + 1) * per] = gathered[place, per:2 * per]

    @pl.loop(0, chunks)
    def _(c):
        await_bytes(arrived.at[c, pl.ds(0, (n - 1) * pad)], fwd_recv.at[c])
        tail = pad - 16
        spot = lax.broadcasted_iota(jnp.int32, (16, channels), 0)

        @pl.loop(0, n)
        def _(d):
            after = pl.multiple_of(lax.rem(d + 1, n) * pad, 16)
            before = pl.multiple_of(lax.rem(d + n - 1, n) * pad + tail, 16)
            here = pl.ds(pl.multiple_of(d * pad + tail, 16), 16)
            first = arrived[c, pl.ds(after, 16)].astype(jnp.float32)
            last = arrived[c, pl.ds(before, 16)].astype(jnp.float32)
            block = arrived[c, here].astype(jnp.float32)
            block = jnp.where(spot == own - tail, pltpu.roll(first, own - tail, 0), block)
            block = jnp.where(spot == 15, pltpu.roll(last, pad - own, 0), block)
            arrived[c, here] = block.astype(jnp.bfloat16)

        whole = arrived[c]
        real = jnp.dot(tf[0:modes], whole, preferred_element_type=jnp.float32) * (1.0 / length)
        imag = jnp.dot(tf[modes:], whole, preferred_element_type=jnp.float32) * (1.0 / length)
        limit = limits[lax.rem(c * n + me, lat_dev)]
        order = lax.broadcasted_iota(jnp.int32, (modes, channels), 0)
        keep = jnp.where(order < limit, jnp.where(order == 0, 1.0, 2.0), 0.0)
        filt[0:modes] = ((wr[...] * real - wi[...] * imag) * keep).astype(jnp.bfloat16)
        filt[modes:] = ((wr[...] * imag + wi[...] * real) * keep).astype(jnp.bfloat16)
        size = PLANE * pad

        @pl.loop(0, groups)
        def _(t):
            target = lax.rem(plane + groups // 2 + t * (groups - 1), groups)
            part = pl.ds(pl.multiple_of(target * size, 16), size)
            here = arrived[c, part]
            spectral = jnp.dot(ti[part], filt[...], preferred_element_type=jnp.float32)
            mixed = jnp.dot(here, mix[...], preferred_element_type=jnp.float32)
            summed = spectral.astype(jnp.bfloat16).astype(jnp.float32) + mixed
            done = here.astype(jnp.float32) + jax.nn.gelu(summed, approximate=True)
            outgoing[pl.ds(c * n + target * PLANE, PLANE)] = done.astype(
                jnp.bfloat16
            ).reshape(PLANE, pad, channels)

            @pl.loop(0, PLANE)
            def _(q):
                to = target * PLANE + lax.rem(mine + q, PLANE)

                @pl.when(to != me)
                def _():
                    send(
                        outgoing.at[c * n + to], lo.at[c * n + me],
                        ret_send, ret_recv.at[c * n + me], to,
                    ).start()

        lo[c * n + me] = outgoing[c * n + me]

    def await_row(r):
        @pl.when(lax.rem(r, n) != me)
        def _():
            await_bytes(lo.at[r], ret_recv.at[r])

    half = channels // 2

    def keep_row(r, j):
        for s, part in enumerate(lanes):
            row = lo[r, :, part].astype(jnp.float32)[0:own]
            staged[s, pl.ds(j, own, stride=lat_dev), :] = row

    def keep_member(m):
        start = pl.multiple_of(m * cells, 8)
        for s, part in enumerate(lanes):
            lo_rows[pl.ds(start, cells), part] = staged[s, 0:cells].astype(jnp.bfloat16)

    if fused:
        squares[...] = jnp.zeros_like(squares)

        def residual(m, j):
            r = m * lat_dev + j
            zonal = lo[r, :, 0:half].astype(jnp.float32)
            zonal = (pltpu.roll(zonal, pad - 1, 0) - pltpu.roll(zonal, 1, 0)) * slope
            north = lo[m * lat_dev + jnp.minimum(j + 1, lat_dev - 1), :, half:].astype(jnp.float32)
            south = lo[m * lat_dev + jnp.maximum(j - 1, 0), :, half:].astype(jnp.float32)
            merid = (north * cosines[pl.ds(j + 2, 1)] - south * cosines[pl.ds(j, 1)]) * polar
            flow = (zonal + merid)[0:own]
            spread = pl.ds(m * cells + j, own, stride=lat_dev)
            value = flow + cosines[pl.ds(j + 1, 1)] * force[spread, :]
            value = ocean[j] * value
            raw[spread, :] = value
            return value * value

        step = 2 if lat_dev % 2 == 0 else 1

        @pl.loop(0, members)
        def _(m):
            await_row(m * lat_dev)

            @pl.loop(0, lat_dev, step=step)
            def _(j):
                for k in range(1, step):
                    await_row(m * lat_dev + j + k)

                @pl.when(j + step < lat_dev)
                def _():
                    await_row(m * lat_dev + j + step)

                total = residual(m, j)
                keep_row(m * lat_dev + j, j)
                for k in range(1, step):
                    total += residual(m, j + k)
                    keep_row(m * lat_dev + j + k, j + k)
                squares[...] += total

            keep_member(m)

        sums[me] = jnp.broadcast_to(
            jnp.sum(squares[...], axis=0, keepdims=True) * 0.125, (8, half)
        )

        @pl.loop(1, n)
        def _(i):
            to = lax.rem(me + i, n)
            send(sums.at[me], sums.at[me], sum_send, sum_recv, to).start()

        await_bytes(sums.at[pl.ds(0, n - 1)], sum_recv)
        total = jnp.sum(sums[...], axis=0)
        total = jnp.sum(jnp.sum(total, axis=0, keepdims=True), axis=1, keepdims=True)
        scale = 1.0 / (rows * own * n * half)
        inverse = 1.0 / jnp.sqrt(total * scale + 1e-06)

        step = lat_dev * own // 5

        @pl.loop(0, 5 * members)
        def _(r):
            part = pl.ds(pl.multiple_of(r * step, 8), step)
            raw[part] = raw[part] * inverse

        await_bytes(sums.at[pl.ds(0, n - 1)], sum_send)
    else:
        @pl.loop(0, members)
        def _(m):
            @pl.loop(0, lat_dev)
            def _(j):
                await_row(m * lat_dev + j)
                keep_row(m * lat_dev + j, j)

            keep_member(m)

    for c in range(max(chunks - 2, 0), chunks):
        await_bytes(fields.at[pl.ds(0, n - 1)], fwd_send.at[c])
    await_bytes(outgoing.at[pl.ds(0, chunks * (n - 1))], ret_send)
    if groups > 1:
        await_bytes(gathered.at[pl.ds(0, groups - 1)], gat_send.at[0])
    await_bytes(gathered.at[pl.ds(0, (PLANE - 1) * groups)], gat_send.at[1])


def extended(block, axis, dim):
    count = lax.axis_size(axis)
    forward = [(i, i + 1) for i in range(count - 1)]
    if axis == "lon":
        forward.append((count - 1, 0))
    backward = [(target, source) for source, target in forward]
    low = lax.ppermute(lax.slice_in_dim(block, block.shape[dim] - 1, None, axis=dim), axis, forward)
    high = lax.ppermute(lax.slice_in_dim(block, 0, 1, axis=dim), axis, backward)
    return jnp.concatenate([low, block, high], axis=dim)


def per_device(fields, mix_weight, spectral_weight, mode_limit, land_mask, forcing):
    members, lat_dev, own, channels = fields.shape
    half = channels // 2
    n = lax.axis_size("lon")
    lat_count = lax.axis_size("lat")
    length = own * n
    nlat = lat_dev * lat_count
    rows = members * lat_dev
    chunks = rows // n
    per = spectral_weight.shape[1]
    modes = per * n
    pad = -(-(own + 2) // 16) * 16
    fused = lat_count == 1
    forward, inverse = tables(length, modes, n, pad)
    slope = length / (4.0 * math.pi)
    polar = nlat / (2.0 * math.pi)
    cells = own * lat_dev

    def by_longitude(array):
        return array.transpose(0, 2, 1, 3).reshape(members * cells, array.shape[3])

    def by_latitude(array):
        shape = (members, own, lat_dev, array.shape[1])
        return array.reshape(shape).transpose(0, 2, 1, 3)

    vmem = pl.BlockSpec(memory_space=pltpu.VMEM)
    away = pl.BlockSpec(memory_space=pltpu.HBM)
    operands = [by_longitude(fields).reshape(members, cells, channels), mix_weight, spectral_weight.transpose(1, 0, 2), mode_limit,
                jnp.asarray(forward), jnp.asarray(inverse)]
    in_specs = [away] * 6
    out_shape = [jax.ShapeDtypeStruct((members * cells, channels), jnp.bfloat16)]
    if fused:
        latitude = np.float32(-0.5 * math.pi) + (
            np.arange(nlat, dtype=np.float32) + np.float32(0.5)
        ) * np.float32(math.pi / nlat)
        cosines = np.zeros((nlat + 2, half), np.float32)
        cosines[1:-1] = np.cos(latitude)[:, None]
        operands += [by_longitude(forcing), land_mask, jnp.asarray(cosines)]
        in_specs += [away] * 3
        out_shape += [
            jax.ShapeDtypeStruct((members * cells, half), jnp.float32),
        ]
    gat_rows = -(-2 * per // 8) * 8
    dma = pltpu.SemaphoreType.DMA
    results = pl.pallas_call(
        functools.partial(
            layer_kernel, n, lat_dev, own, length, slope, polar, fused
        ),
        out_shape=out_shape,
        in_specs=in_specs,
        out_specs=[vmem] * len(out_shape),
        scratch_shapes=[
            pltpu.VMEM((members, cells, channels), jnp.bfloat16),
            pltpu.VMEM(mix_weight.shape, jnp.bfloat16),
            pltpu.VMEM((per, 2, channels), jnp.float32),
            pltpu.SMEM(mode_limit.shape, jnp.int32),
            pltpu.VMEM(land_mask.shape, jnp.int32),
            pltpu.VMEM((nlat + 2, half), jnp.float32),
            pltpu.VMEM((lat_dev, own, half), jnp.float32),
            pltpu.VMEM((rows, pad, channels), jnp.bfloat16),
            pltpu.VMEM((channels // 128, pad * lat_dev, 128), jnp.float32),
            pltpu.VMEM((rows, pad, channels), jnp.bfloat16),
            pltpu.VMEM((n, gat_rows, channels), jnp.float32),
            pltpu.VMEM((modes, channels), jnp.float32),
            pltpu.VMEM((modes, channels), jnp.float32),
            pltpu.VMEM((chunks, n * pad, channels), jnp.bfloat16),
            pltpu.VMEM((2 * modes, channels), jnp.bfloat16),
            pltpu.VMEM((rows, pad, channels), jnp.bfloat16),
            pltpu.VMEM(forward.shape, jnp.bfloat16),
            pltpu.VMEM(inverse.shape, jnp.bfloat16),
            pltpu.VMEM((members * cells, half) if fused else (8, half), jnp.float32),
            pltpu.VMEM((n, 8, half), jnp.float32),
            pltpu.VMEM((own, half), jnp.float32),
            dma((chunks,)), dma((chunks,)), dma, dma((rows,)), dma((2,)), dma((2,)),
            dma((members + 8,)), dma, dma,
        ],
        compiler_params=pltpu.CompilerParams(
            collective_id=0, has_side_effects=True, vmem_limit_bytes=40 * 2**20
        ),
    )(*operands)
    layer_out = by_latitude(results[0])
    if fused:
        residual = by_latitude(results[1])
        return layer_out, residual
    zonal = extended(layer_out[..., :half], "lon", 2).astype(jnp.float32)
    zonal = (zonal[:, :, 2:] - zonal[:, :, :-2]) * slope
    merid = extended(layer_out[..., half:], "lat", 1).astype(jnp.float32)
    lat_ids = lax.axis_index("lat") * lat_dev + jnp.arange(-1, lat_dev + 1, dtype=jnp.int32)
    latitude = -0.5 * math.pi + (lat_ids.astype(jnp.float32) + 0.5) * (math.pi / nlat)
    cos_lat = jnp.cos(latitude)
    weighted = merid * cos_lat[None, :, None, None]
    merid = (weighted[:, 2:] - weighted[:, :-2]) * polar
    ocean = land_mask.astype(jnp.float32)[None, :, :, None]
    raw = ocean * (zonal + merid + cos_lat[1:-1][None, :, None, None] * forcing)
    total = lax.psum(jnp.sum(raw * raw), ("lon", "lat"))
    norm = jnp.sqrt(total / (members * nlat * length * half) + 1e-06)
    return layer_out, raw / norm


def solution(mesh):
    placed = (
        P(None, "lat", "lon", None),
        P(),
        P(None, "lon", None),
        P("lat"),
        P("lat", "lon"),
        P(None, "lat", "lon", None),
    )
    return jax.shard_map(
        per_device,
        mesh=mesh,
        in_specs=placed,
        out_specs=(P(None, "lat", "lon", None), P(None, "lat", "lon", None)),
        check_vma=False,
    )
```

```python
import functools
import math

import jax
import jax.numpy as jnp
import numpy as np
from jax import lax
from jax.experimental import pallas as pl
from jax.experimental.pallas import tpu as pltpu
from jax.sharding import PartitionSpec as P

MESH = pl.DeviceIdType.MESH
PLANE = 8


def tables(length, wavenumbers, count, pad):
    own = length // count
    places = np.arange(count)[:, None] * own + np.arange(pad)[None, :]
    places[:, pad - 1] = np.arange(count) * own - 1
    places = places % length
    order = np.arange(wavenumbers)[:, None, None]
    angles = (order * places[None] % length).astype(np.float32) * np.float32(
        2.0 * math.pi / length
    )
    full = np.concatenate([np.cos(angles), -np.sin(angles)], axis=0)
    inverse = full.reshape(2 * wavenumbers, count * pad).T.astype(jnp.bfloat16)
    full[:, :, own:] = 0.0
    forward = full.reshape(2 * wavenumbers, count * pad)
    return forward.astype(jnp.bfloat16), inverse


def layer_kernel(
    n, lat_dev, own, length, slope, polar, fused,
    fields_in, mix_in, weight_in, limits_in, table_f, table_i, *rest,
):
    if fused:
        forcing, mask_in, cos_in, lo_rows, raw = rest[:5]
        rest = rest[5:]
    else:
        lo_rows = rest[0]
        rest = rest[1:]
    (native, mix, weight, limits, mask, cosines, ocean, fields, staged, lo, gathered, wr, wi, arrived, filt, outgoing, tf, ti,
     force, sums, squares,
     fwd_send, fwd_recv, ret_send, ret_recv, gat_send, gat_recv,
     local_sem, sum_send, sum_recv) = rest
    rows, pad, channels = fields.shape
    chunks = rows // n
    members = rows // lat_dev
    cells = own * lat_dev
    per = weight.shape[0]
    modes = per * n
    me = lax.axis_index("lon")
    groups = n // PLANE
    mine = lax.rem(me, PLANE)
    plane = me // PLANE
    stride = n // 3 + 1
    while math.gcd(stride, n) > 1:
        stride += 1

    def send(src, dst, s_sem, r_sem, to):
        return pltpu.make_async_remote_copy(
            src_ref=src, dst_ref=dst, send_sem=s_sem, recv_sem=r_sem,
            device_id={"lon": to}, device_id_type=MESH,
        )

    def await_bytes(ref, sem):
        pltpu.make_async_copy(ref, ref, sem).wait()

    barrier = pltpu.get_barrier_semaphore()

    @pl.loop(1, n)
    def _(i):
        pl.semaphore_signal(
            barrier, inc=1, device_id={"lon": lax.rem(me + i, n)}, device_id_type=MESH
        )

    pairs = [(weight_in, weight)]
    for m in range(members):
        pairs.append((fields_in.at[m], native.at[m]))
    pairs += [(table_f, tf), (table_i, ti), (mix_in, mix), (limits_in, limits)]
    if fused:
        pairs += [(mask_in, mask), (cos_in, cosines), (forcing, force)]
    loads = [
        pltpu.make_async_copy(src, dst, local_sem.at[i]) for i, (src, dst) in enumerate(pairs)
    ]
    for load in loads:
        load.start()
    loads[0].wait()

    slot = mine * groups + plane
    gathered[slot, 0:per] = weight[:, 0]
    gathered[slot, per:2 * per] = weight[:, 1]
    lanes = [slice(part, part + 128) for part in range(0, channels, 128)]
    for s in range(len(lanes)):
        staged[s, cells:] = jnp.zeros(((pad - own) * lat_dev, 128), jnp.float32)

    def prepare(m):
        loads[1 + m].wait()
        for s, part in enumerate(lanes):
            staged[s, 0:cells] = native[m, :, part].astype(jnp.float32)

        @pl.loop(0, lat_dev)
        def _(j):
            for s, part in enumerate(lanes):
                row = staged[s, pl.ds(j, pad, stride=lat_dev), :]
                fields[m * lat_dev + j, :, part] = row.astype(jnp.bfloat16)

    ready = 0
    while ready < members and ready * lat_dev < n:
        prepare(ready)
        ready += 1
    pl.semaphore_wait(barrier, n - 1)

    @pl.loop(1, groups)
    def _(i):
        to = lax.rem(plane + i, groups) * PLANE + mine
        send(gathered.at[slot], gathered.at[slot], gat_send.at[0], gat_recv.at[0], to).start()

    def scatter(c):
        @pl.loop(1, n)
        def _(i):
            to = lax.rem(me + lax.rem(i * stride, n), n)
            place = pl.multiple_of(me * pad, 16)
            send(
                fields.at[c * n + to], arrived.at[c, pl.ds(place, pad)],
                fwd_send.at[c], fwd_recv.at[c], to,
            ).start()

        place = pl.multiple_of(me * pad, 16)
        arrived[c, pl.ds(place, pad)] = fields[c * n + me]

    scatter(0)
    if groups > 1:
        await_bytes(gathered.at[pl.ds(0, groups - 1)], gat_recv.at[0])
    held = gathered.at[pl.ds(mine * groups, groups)]

    @pl.loop(1, PLANE)
    def _(i):
        to = plane * PLANE + lax.rem(mine + i, PLANE)
        send(held, held, gat_send.at[1], gat_recv.at[1], to).start()

    for c in range(1, chunks):
        while ready < members and ready * lat_dev < (c + 1) * n:
            prepare(ready)
            ready += 1
        if c >= 2:
            await_bytes(fields.at[pl.ds(0, n - 1)], fwd_send.at[c - 2])
        scatter(c)

    for load in loads[1 + members:]:
        load.wait()
    if fused:
        eye = [lax.broadcasted_iota(jnp.int32, (own, own), k) for k in range(2)]
        eye = (eye[0] == eye[1]).astype(jnp.bfloat16)
        turned = lax.dot_general(
            eye, mask[...].astype(jnp.float32).astype(jnp.bfloat16), (((1,), (1,)), ((), ())),
            preferred_element_type=jnp.float32,
        ).astype(jnp.bfloat16)
        row_of = lax.broadcasted_iota(jnp.int32, (lat_dev, channels // 2), 0)

        @pl.loop(0, lat_dev)
        def _(j):
            chosen = (row_of == j).astype(jnp.float32).astype(jnp.bfloat16)
            ocean[j] = jnp.dot(turned, chosen, preferred_element_type=jnp.float32)

    await_bytes(gathered.at[pl.ds(0, n - groups)], gat_recv.at[1])
    for device in range(n):
        place = (device % PLANE) * groups + device // PLANE
        wr[device * per:(device + 1) * per] = gathered[place, 0:per]
        wi[device * per:(device + 1) * per] = gathered[place, per:2 * per]

    @pl.loop(0, chunks)
    def _(c):
        await_bytes(arrived.at[c, pl.ds(0, (n - 1) * pad)], fwd_recv.at[c])
        tail = pad - 16
        spot = lax.broadcasted_iota(jnp.int32, (16, channels), 0)

        @pl.loop(0, n)
        def _(d):
            after = pl.multiple_of(lax.rem(d + 1, n) * pad, 16)
            before = pl.multiple_of(lax.rem(d + n - 1, n) * pad + tail, 16)
            here = pl.ds(pl.multiple_of(d * pad + tail, 16), 16)
            first = arrived[c, pl.ds(after, 16)].astype(jnp.float32)
            last = arrived[c, pl.ds(before, 16)].astype(jnp.float32)
            block = arrived[c, here].astype(jnp.float32)
            block = jnp.where(spot == own - tail, pltpu.roll(first, own - tail, 0), block)
            block = jnp.where(spot == 15, pltpu.roll(last, pad - own, 0), block)
            arrived[c, here] = block.astype(jnp.bfloat16)

        whole = arrived[c]
        real = jnp.dot(tf[0:modes], whole, preferred_element_type=jnp.float32) * (1.0 / length)
        imag = jnp.dot(tf[modes:], whole, preferred_element_type=jnp.float32) * (1.0 / length)
        limit = limits[lax.rem(c * n + me, lat_dev)]
        order = lax.broadcasted_iota(jnp.int32, (modes, channels), 0)
        keep = jnp.where(order < limit, jnp.where(order == 0, 1.0, 2.0), 0.0)
        filt[0:modes] = ((wr[...] * real - wi[...] * imag) * keep).astype(jnp.bfloat16)
        filt[modes:] = ((wr[...] * imag + wi[...] * real) * keep).astype(jnp.bfloat16)
        size = PLANE * pad

        @pl.loop(0, groups)
        def _(t):
            target = lax.rem(plane + groups // 2 + t * (groups - 1), groups)
            part = pl.ds(pl.multiple_of(target * size, 16), size)
            here = arrived[c, part]
            spectral = jnp.dot(ti[part], filt[...], preferred_element_type=jnp.float32)
            mixed = jnp.dot(here, mix[...], preferred_element_type=jnp.float32)
            summed = spectral.astype(jnp.bfloat16).astype(jnp.float32) + mixed
            done = here.astype(jnp.float32) + jax.nn.gelu(summed, approximate=True)
            outgoing[pl.ds(c * n + target * PLANE, PLANE)] = done.astype(
                jnp.bfloat16
            ).reshape(PLANE, pad, channels)

            @pl.loop(0, PLANE)
            def _(q):
                to = target * PLANE + lax.rem(mine + q, PLANE)

                @pl.when(to != me)
                def _():
                    send(
                        outgoing.at[c * n + to], lo.at[c * n + me],
                        ret_send, ret_recv.at[c * n + me], to,
                    ).start()

        lo[c * n + me] = outgoing[c * n + me]

    def await_row(r):
        @pl.when(lax.rem(r, n) != me)
        def _():
            await_bytes(lo.at[r], ret_recv.at[r])

    half = channels // 2

    def keep_row(r, j):
        for s, part in enumerate(lanes):
            row = lo[r, :, part].astype(jnp.float32)[0:own]
            staged[s, pl.ds(j, own, stride=lat_dev), :] = row

    def keep_member(m):
        start = pl.multiple_of(m * cells, 8)
        for s, part in enumerate(lanes):
            lo_rows[pl.ds(start, cells), part] = staged[s, 0:cells].astype(jnp.bfloat16)

    if fused:
        squares[...] = jnp.zeros_like(squares)

        def residual(m, j):
            r = m * lat_dev + j
            zonal = lo[r, :, 0:half].astype(jnp.float32)
            zonal = (pltpu.roll(zonal, pad - 1, 0) - pltpu.roll(zonal, 1, 0)) * slope
            north = lo[m * lat_dev + jnp.minimum(j + 1, lat_dev - 1), :, half:].astype(jnp.float32)
            south = lo[m * lat_dev + jnp.maximum(j - 1, 0), :, half:].astype(jnp.float32)
            merid = (north * cosines[pl.ds(j + 2, 1)] - south * cosines[pl.ds(j, 1)]) * polar
            flow = (zonal + merid)[0:own]
            spread = pl.ds(m * cells + j, own, stride=lat_dev)
            value = flow + cosines[pl.ds(j + 1, 1)] * force[spread, :]
            value = ocean[j] * value
            raw[spread, :] = value
            return value * value

        step = 2 if lat_dev % 2 == 0 else 1

        @pl.loop(0, members)
        def _(m):
            await_row(m * lat_dev)

            @pl.loop(0, lat_dev, step=step)
            def _(j):
                for k in range(1, step):
                    await_row(m * lat_dev + j + k)

                @pl.when(j + step < lat_dev)
                def _():
                    await_row(m * lat_dev + j + step)

                total = residual(m, j)
                keep_row(m * lat_dev + j, j)
                for k in range(1, step):
                    total += residual(m, j + k)
                    keep_row(m * lat_dev + j + k, j + k)
                squares[...] += total

            keep_member(m)

        sums[me] = jnp.broadcast_to(
            jnp.sum(squares[...], axis=0, keepdims=True) * 0.125, (8, half)
        )

        @pl.loop(1, n)
        def _(i):
            to = lax.rem(me + i, n)
            send(sums.at[me], sums.at[me], sum_send, sum_recv, to).start()

        await_bytes(sums.at[pl.ds(0, n - 1)], sum_recv)
        total = jnp.sum(sums[...], axis=0)
        total = jnp.sum(jnp.sum(total, axis=0, keepdims=True), axis=1, keepdims=True)
        scale = 1.0 / (rows * own * n * half)
        inverse = 1.0 / jnp.sqrt(total * scale + 1e-06)

        step = lat_dev * own // 5

        @pl.loop(0, 5 * members)
        def _(r):
            part = pl.ds(pl.multiple_of(r * step, 8), step)
            raw[part] = raw[part] * inverse

        await_bytes(sums.at[pl.ds(0, n - 1)], sum_send)
    else:
        @pl.loop(0, members)
        def _(m):
            @pl.loop(0, lat_dev)
            def _(j):
                await_row(m * lat_dev + j)
                keep_row(m * lat_dev + j, j)

            keep_member(m)

    for c in range(max(chunks - 2, 0), chunks):
        await_bytes(fields.at[pl.ds(0, n - 1)], fwd_send.at[c])
    await_bytes(outgoing.at[pl.ds(0, chunks * (n - 1))], ret_send)
    if groups > 1:
        await_bytes(gathered.at[pl.ds(0, groups - 1)], gat_send.at[0])
    await_bytes(gathered.at[pl.ds(0, (PLANE - 1) * groups)], gat_send.at[1])


def extended(block, axis, dim):
    count = lax.axis_size(axis)
    forward = [(i, i + 1) for i in range(count - 1)]
    if axis == "lon":
        forward.append((count - 1, 0))
    backward = [(target, source) for source, target in forward]
    low = lax.ppermute(lax.slice_in_dim(block, block.shape[dim] - 1, None, axis=dim), axis, forward)
    high = lax.ppermute(lax.slice_in_dim(block, 0, 1, axis=dim), axis, backward)
    return jnp.concatenate([low, block, high], axis=dim)


def per_device(fields, mix_weight, spectral_weight, mode_limit, land_mask, forcing):
    members, lat_dev, own, channels = fields.shape
    half = channels // 2
    n = lax.axis_size("lon")
    lat_count = lax.axis_size("lat")
    length = own * n
    nlat = lat_dev * lat_count
    rows = members * lat_dev
    chunks = rows // n
    per = spectral_weight.shape[1]
    modes = per * n
    pad = -(-(own + 2) // 16) * 16
    fused = lat_count == 1
    forward, inverse = tables(length, modes, n, pad)
    slope = length / (4.0 * math.pi)
    polar = nlat / (2.0 * math.pi)
    cells = own * lat_dev

    def by_longitude(array):
        return array.transpose(0, 2, 1, 3).reshape(members * cells, array.shape[3])

    def by_latitude(array):
        shape = (members, own, lat_dev, array.shape[1])
        return array.reshape(shape).transpose(0, 2, 1, 3)

    vmem = pl.BlockSpec(memory_space=pltpu.VMEM)
    away = pl.BlockSpec(memory_space=pltpu.HBM)
    operands = [by_longitude(fields).reshape(members, cells, channels), mix_weight, spectral_weight.transpose(1, 0, 2), mode_limit,
                jnp.asarray(forward), jnp.asarray(inverse)]
    in_specs = [away] * 6
    out_shape = [jax.ShapeDtypeStruct((members * cells, channels), jnp.bfloat16)]
    if fused:
        latitude = np.float32(-0.5 * math.pi) + (
            np.arange(nlat, dtype=np.float32) + np.float32(0.5)
        ) * np.float32(math.pi / nlat)
        cosines = np.zeros((nlat + 2, half), np.float32)
        cosines[1:-1] = np.cos(latitude)[:, None]
        operands += [by_longitude(forcing), land_mask, jnp.asarray(cosines)]
        in_specs += [away] * 3
        out_shape += [
            jax.ShapeDtypeStruct((members * cells, half), jnp.float32),
        ]
    gat_rows = -(-2 * per // 8) * 8
    dma = pltpu.SemaphoreType.DMA
    results = pl.pallas_call(
        functools.partial(
            layer_kernel, n, lat_dev, own, length, slope, polar, fused
        ),
        out_shape=out_shape,
        in_specs=in_specs,
        out_specs=[vmem] * len(out_shape),
        scratch_shapes=[
            pltpu.VMEM((members, cells, channels), jnp.bfloat16),
            pltpu.VMEM(mix_weight.shape, jnp.bfloat16),
            pltpu.VMEM((per, 2, channels), jnp.float32),
            pltpu.SMEM(mode_limit.shape, jnp.int32),
            pltpu.VMEM(land_mask.shape, jnp.int32),
            pltpu.VMEM((nlat + 2, half), jnp.float32),
            pltpu.VMEM((lat_dev, own, half), jnp.float32),
            pltpu.VMEM((rows, pad, channels), jnp.bfloat16),
            pltpu.VMEM((channels // 128, pad * lat_dev, 128), jnp.float32),
            pltpu.VMEM((rows, pad, channels), jnp.bfloat16),
            pltpu.VMEM((n, gat_rows, channels), jnp.float32),
            pltpu.VMEM((modes, channels), jnp.float32),
            pltpu.VMEM((modes, channels), jnp.float32),
            pltpu.VMEM((chunks, n * pad, channels), jnp.bfloat16),
            pltpu.VMEM((2 * modes, channels), jnp.bfloat16),
            pltpu.VMEM((rows, pad, channels), jnp.bfloat16),
            pltpu.VMEM(forward.shape, jnp.bfloat16),
            pltpu.VMEM(inverse.shape, jnp.bfloat16),
            pltpu.VMEM((members * cells, half) if fused else (8, half), jnp.float32),
            pltpu.VMEM((n, 8, half), jnp.float32),
            pltpu.VMEM((own, half), jnp.float32),
            dma((chunks,)), dma((chunks,)), dma, dma((rows,)), dma((2,)), dma((2,)),
            dma((members + 8,)), dma, dma,
        ],
        compiler_params=pltpu.CompilerParams(
            collective_id=0, has_side_effects=True, vmem_limit_bytes=62 * 2**20
        ),
    )(*operands)
    layer_out = by_latitude(results[0])
    if fused:
        residual = by_latitude(results[1])
        return layer_out, residual
    zonal = extended(layer_out[..., :half], "lon", 2).astype(jnp.float32)
    zonal = (zonal[:, :, 2:] - zonal[:, :, :-2]) * slope
    merid = extended(layer_out[..., half:], "lat", 1).astype(jnp.float32)
    lat_ids = lax.axis_index("lat") * lat_dev + jnp.arange(-1, lat_dev + 1, dtype=jnp.int32)
    latitude = -0.5 * math.pi + (lat_ids.astype(jnp.float32) + 0.5) * (math.pi / nlat)
    cos_lat = jnp.cos(latitude)
    weighted = merid * cos_lat[None, :, None, None]
    merid = (weighted[:, 2:] - weighted[:, :-2]) * polar
    ocean = land_mask.astype(jnp.float32)[None, :, :, None]
    raw = ocean * (zonal + merid + cos_lat[1:-1][None, :, None, None] * forcing)
    total = lax.psum(jnp.sum(raw * raw), ("lon", "lat"))
    norm = jnp.sqrt(total / (members * nlat * length * half) + 1e-06)
    return layer_out, raw / norm


def solution(mesh):
    placed = (
        P(None, "lat", "lon", None),
        P(),
        P(None, "lon", None),
        P("lat"),
        P("lat", "lon"),
        P(None, "lat", "lon", None),
    )
    return jax.shard_map(
        per_device,
        mesh=mesh,
        in_specs=placed,
        out_specs=(P(None, "lat", "lon", None), P(None, "lat", "lon", None)),
        check_vma=False,
    )
```

```python
import functools
import math

import jax
import jax.numpy as jnp
import numpy as np
from jax import lax
from jax.experimental import pallas as pl
from jax.experimental.pallas import tpu as pltpu
from jax.sharding import PartitionSpec as P

MESH = pl.DeviceIdType.MESH
PLANE = 8


def tables(length, wavenumbers, count, pad):
    own = length // count
    places = np.arange(count)[:, None] * own + np.arange(pad)[None, :]
    places[:, pad - 1] = np.arange(count) * own - 1
    places = places % length
    order = np.arange(wavenumbers)[:, None, None]
    angles = (order * places[None] % length).astype(np.float32) * np.float32(
        2.0 * math.pi / length
    )
    full = np.concatenate([np.cos(angles), -np.sin(angles)], axis=0)
    inverse = full.reshape(2 * wavenumbers, count * pad).T.astype(jnp.bfloat16)
    full[:, :, own:] = 0.0
    forward = full.reshape(2 * wavenumbers, count * pad)
    return forward.astype(jnp.bfloat16), inverse


def layer_kernel(
    n, lat_dev, own, length, slope, polar, fused,
    fields_in, mix_in, weight_in, limits_in, table_f, table_i, *rest,
):
    if fused:
        forcing, mask_in, cos_in, lo_rows, raw = rest[:5]
        rest = rest[5:]
    else:
        lo_rows = rest[0]
        rest = rest[1:]
    (kept, out_sem, native, mix, weight, limits, mask, cosines, ocean, fields, staged, lo, gathered, wr, wi, arrived, filt, outgoing, tf, ti,
     force, sums, squares,
     fwd_send, fwd_recv, ret_send, ret_recv, gat_send, gat_recv,
     local_sem, sum_send, sum_recv) = rest
    rows, pad, channels = fields.shape
    chunks = rows // n
    members = rows // lat_dev
    cells = own * lat_dev
    per = weight.shape[0]
    modes = per * n
    me = lax.axis_index("lon")
    groups = n // PLANE
    mine = lax.rem(me, PLANE)
    plane = me // PLANE
    stride = n // 3 + 1
    while math.gcd(stride, n) > 1:
        stride += 1

    def send(src, dst, s_sem, r_sem, to):
        return pltpu.make_async_remote_copy(
            src_ref=src, dst_ref=dst, send_sem=s_sem, recv_sem=r_sem,
            device_id={"lon": to}, device_id_type=MESH,
        )

    def await_bytes(ref, sem):
        pltpu.make_async_copy(ref, ref, sem).wait()

    barrier = pltpu.get_barrier_semaphore()

    @pl.loop(1, n)
    def _(i):
        pl.semaphore_signal(
            barrier, inc=1, device_id={"lon": lax.rem(me + i, n)}, device_id_type=MESH
        )

    pairs = [(weight_in, weight)]
    for m in range(members):
        pairs.append((fields_in.at[m], native.at[m]))
    pairs += [(table_f, tf), (table_i, ti), (mix_in, mix), (limits_in, limits)]
    if fused:
        pairs += [(mask_in, mask), (cos_in, cosines), (forcing, force)]
    loads = [
        pltpu.make_async_copy(src, dst, local_sem.at[i]) for i, (src, dst) in enumerate(pairs)
    ]
    for load in loads[:1 + members]:
        load.start()
    loads[0].wait()

    slot = mine * groups + plane
    gathered[slot, 0:per] = weight[:, 0]
    gathered[slot, per:2 * per] = weight[:, 1]
    lanes = [slice(part, part + 128) for part in range(0, channels, 128)]
    for s in range(len(lanes)):
        staged[s, cells:] = jnp.zeros(((pad - own) * lat_dev, 128), jnp.float32)

    def prepare(m):
        loads[1 + m].wait()
        for s, part in enumerate(lanes):
            staged[s, 0:cells] = native[m, :, part].astype(jnp.float32)

        @pl.loop(0, lat_dev)
        def _(j):
            for s, part in enumerate(lanes):
                row = staged[s, pl.ds(j, pad, stride=lat_dev), :]
                fields[m * lat_dev + j, :, part] = row.astype(jnp.bfloat16)

    ready = 0
    while ready < members and ready * lat_dev < n:
        prepare(ready)
        ready += 1
    pl.semaphore_wait(barrier, n - 1)

    @pl.loop(1, groups)
    def _(i):
        to = lax.rem(plane + i, groups) * PLANE + mine
        send(gathered.at[slot], gathered.at[slot], gat_send.at[0], gat_recv.at[0], to).start()

    def scatter(c):
        @pl.loop(1, n)
        def _(i):
            to = lax.rem(me + lax.rem(i * stride, n), n)
            place = pl.multiple_of(me * pad, 16)
            send(
                fields.at[c * n + to], arrived.at[c, pl.ds(place, pad)],
                fwd_send.at[c], fwd_recv.at[c], to,
            ).start()

        place = pl.multiple_of(me * pad, 16)
        arrived[c, pl.ds(place, pad)] = fields[c * n + me]

    scatter(0)
    for load in loads[1 + members:]:
        load.start()
    if groups > 1:
        await_bytes(gathered.at[pl.ds(0, groups - 1)], gat_recv.at[0])
    held = gathered.at[pl.ds(mine * groups, groups)]

    @pl.loop(1, PLANE)
    def _(i):
        to = plane * PLANE + lax.rem(mine + i, PLANE)
        send(held, held, gat_send.at[1], gat_recv.at[1], to).start()

    for c in range(1, chunks):
        while ready < members and ready * lat_dev < (c + 1) * n:
            prepare(ready)
            ready += 1
        if c >= 2:
            await_bytes(fields.at[pl.ds(0, n - 1)], fwd_send.at[c - 2])
        scatter(c)

    for load in loads[1 + members:]:
        load.wait()
    if fused:
        eye = [lax.broadcasted_iota(jnp.int32, (own, own), k) for k in range(2)]
        eye = (eye[0] == eye[1]).astype(jnp.bfloat16)
        turned = lax.dot_general(
            eye, mask[...].astype(jnp.float32).astype(jnp.bfloat16), (((1,), (1,)), ((), ())),
            preferred_element_type=jnp.float32,
        ).astype(jnp.bfloat16)
        row_of = lax.broadcasted_iota(jnp.int32, (lat_dev, channels // 2), 0)

        @pl.loop(0, lat_dev)
        def _(j):
            chosen = (row_of == j).astype(jnp.float32).astype(jnp.bfloat16)
            ocean[j] = jnp.dot(turned, chosen, preferred_element_type=jnp.float32)

    await_bytes(gathered.at[pl.ds(0, n - groups)], gat_recv.at[1])
    for device in range(n):
        place = (device % PLANE) * groups + device // PLANE
        wr[device * per:(device + 1) * per] = gathered[place, 0:per]
        wi[device * per:(device + 1) * per] = gathered[place, per:2 * per]

    @pl.loop(0, chunks)
    def _(c):
        await_bytes(arrived.at[c, pl.ds(0, (n - 1) * pad)], fwd_recv.at[c])
        tail = pad - 16
        spot = lax.broadcasted_iota(jnp.int32, (16, channels), 0)

        @pl.loop(0, n)
        def _(d):
            after = pl.multiple_of(lax.rem(d + 1, n) * pad, 16)
            before = pl.multiple_of(lax.rem(d + n - 1, n) * pad + tail, 16)
            here = pl.ds(pl.multiple_of(d * pad + tail, 16), 16)
            first = arrived[c, pl.ds(after, 16)].astype(jnp.float32)
            last = arrived[c, pl.ds(before, 16)].astype(jnp.float32)
            block = arrived[c, here].astype(jnp.float32)
            block = jnp.where(spot == own - tail, pltpu.roll(first, own - tail, 0), block)
            block = jnp.where(spot == 15, pltpu.roll(last, pad - own, 0), block)
            arrived[c, here] = block.astype(jnp.bfloat16)

        whole = arrived[c]
        real = jnp.dot(tf[0:modes], whole, preferred_element_type=jnp.float32) * (1.0 / length)
        imag = jnp.dot(tf[modes:], whole, preferred_element_type=jnp.float32) * (1.0 / length)
        limit = limits[lax.rem(c * n + me, lat_dev)]
        order = lax.broadcasted_iota(jnp.int32, (modes, channels), 0)
        keep = jnp.where(order < limit, jnp.where(order == 0, 1.0, 2.0), 0.0)
        filt[0:modes] = ((wr[...] * real - wi[...] * imag) * keep).astype(jnp.bfloat16)
        filt[modes:] = ((wr[...] * imag + wi[...] * real) * keep).astype(jnp.bfloat16)
        size = PLANE * pad

        @pl.loop(0, groups)
        def _(t):
            target = lax.rem(plane + groups // 2 + t * (groups - 1), groups)
            part = pl.ds(pl.multiple_of(target * size, 16), size)
            here = arrived[c, part]
            spectral = jnp.dot(ti[part], filt[...], preferred_element_type=jnp.float32)
            mixed = jnp.dot(here, mix[...], preferred_element_type=jnp.float32)
            summed = spectral.astype(jnp.bfloat16).astype(jnp.float32) + mixed
            done = here.astype(jnp.float32) + jax.nn.gelu(summed, approximate=True)
            outgoing[pl.ds(c * n + target * PLANE, PLANE)] = done.astype(
                jnp.bfloat16
            ).reshape(PLANE, pad, channels)

            @pl.loop(0, PLANE)
            def _(q):
                to = target * PLANE + lax.rem(mine + q, PLANE)

                @pl.when(to != me)
                def _():
                    send(
                        outgoing.at[c * n + to], lo.at[c * n + me],
                        ret_send, ret_recv.at[c * n + me], to,
                    ).start()

        lo[c * n + me] = outgoing[c * n + me]

    def await_row(r):
        @pl.when(lax.rem(r, n) != me)
        def _():
            await_bytes(lo.at[r], ret_recv.at[r])

    half = channels // 2

    def keep_row(r, j):
        for s, part in enumerate(lanes):
            row = lo[r, :, part].astype(jnp.float32)[0:own]
            staged[s, pl.ds(j, own, stride=lat_dev), :] = row

    def keep_member(m):
        for s, part in enumerate(lanes):
            kept[m, :, part] = staged[s, 0:cells].astype(jnp.bfloat16)
        pltpu.make_async_copy(kept.at[m], lo_rows.at[m], out_sem.at[m]).start()

    if fused:
        squares[...] = jnp.zeros_like(squares)

        def residual(m, j):
            r = m * lat_dev + j
            zonal = lo[r, :, 0:half].astype(jnp.float32)
            zonal = (pltpu.roll(zonal, pad - 1, 0) - pltpu.roll(zonal, 1, 0)) * slope
            north = lo[m * lat_dev + jnp.minimum(j + 1, lat_dev - 1), :, half:].astype(jnp.float32)
            south = lo[m * lat_dev + jnp.maximum(j - 1, 0), :, half:].astype(jnp.float32)
            merid = (north * cosines[pl.ds(j + 2, 1)] - south * cosines[pl.ds(j, 1)]) * polar
            flow = (zonal + merid)[0:own]
            spread = pl.ds(m * cells + j, own, stride=lat_dev)
            value = flow + cosines[pl.ds(j + 1, 1)] * force[spread, :]
            value = ocean[j] * value
            raw[spread, :] = value
            return value * value

        step = 2 if lat_dev % 2 == 0 else 1

        @pl.loop(0, members)
        def _(m):
            await_row(m * lat_dev)

            @pl.loop(0, lat_dev, step=step)
            def _(j):
                for k in range(1, step):
                    await_row(m * lat_dev + j + k)

                @pl.when(j + step < lat_dev)
                def _():
                    await_row(m * lat_dev + j + step)

                total = residual(m, j)
                keep_row(m * lat_dev + j, j)
                for k in range(1, step):
                    total += residual(m, j + k)
                    keep_row(m * lat_dev + j + k, j + k)
                squares[...] += total

            keep_member(m)

        sums[me] = jnp.broadcast_to(
            jnp.sum(squares[...], axis=0, keepdims=True) * 0.125, (8, half)
        )

        @pl.loop(1, n)
        def _(i):
            to = lax.rem(me + i, n)
            send(sums.at[me], sums.at[me], sum_send, sum_recv, to).start()

        await_bytes(sums.at[pl.ds(0, n - 1)], sum_recv)
        total = jnp.sum(sums[...], axis=0)
        total = jnp.sum(jnp.sum(total, axis=0, keepdims=True), axis=1, keepdims=True)
        scale = 1.0 / (rows * own * n * half)
        inverse = 1.0 / jnp.sqrt(total * scale + 1e-06)

        step = lat_dev * own // 5

        @pl.loop(0, 5 * members)
        def _(r):
            part = pl.ds(pl.multiple_of(r * step, 8), step)
            raw[part] = raw[part] * inverse

        await_bytes(sums.at[pl.ds(0, n - 1)], sum_send)
    else:
        @pl.loop(0, members)
        def _(m):
            @pl.loop(0, lat_dev)
            def _(j):
                await_row(m * lat_dev + j)
                keep_row(m * lat_dev + j, j)

            keep_member(m)

    for m in range(members):
        pltpu.make_async_copy(kept.at[m], lo_rows.at[m], out_sem.at[m]).wait()
    for c in range(max(chunks - 2, 0), chunks):
        await_bytes(fields.at[pl.ds(0, n - 1)], fwd_send.at[c])
    await_bytes(outgoing.at[pl.ds(0, chunks * (n - 1))], ret_send)
    if groups > 1:
        await_bytes(gathered.at[pl.ds(0, groups - 1)], gat_send.at[0])
    await_bytes(gathered.at[pl.ds(0, (PLANE - 1) * groups)], gat_send.at[1])


def extended(block, axis, dim):
    count = lax.axis_size(axis)
    forward = [(i, i + 1) for i in range(count - 1)]
    if axis == "lon":
        forward.append((count - 1, 0))
    backward = [(target, source) for source, target in forward]
    low = lax.ppermute(lax.slice_in_dim(block, block.shape[dim] - 1, None, axis=dim), axis, forward)
    high = lax.ppermute(lax.slice_in_dim(block, 0, 1, axis=dim), axis, backward)
    return jnp.concatenate([low, block, high], axis=dim)


def per_device(fields, mix_weight, spectral_weight, mode_limit, land_mask, forcing):
    members, lat_dev, own, channels = fields.shape
    half = channels // 2
    n = lax.axis_size("lon")
    lat_count = lax.axis_size("lat")
    length = own * n
    nlat = lat_dev * lat_count
    rows = members * lat_dev
    chunks = rows // n
    per = spectral_weight.shape[1]
    modes = per * n
    pad = -(-(own + 2) // 16) * 16
    fused = lat_count == 1
    forward, inverse = tables(length, modes, n, pad)
    slope = length / (4.0 * math.pi)
    polar = nlat / (2.0 * math.pi)
    cells = own * lat_dev

    def by_longitude(array):
        return array.transpose(0, 2, 1, 3).reshape(members * cells, array.shape[3])

    def by_latitude(array):
        shape = (members, own, lat_dev, array.shape[-1])
        return array.reshape(shape).transpose(0, 2, 1, 3)

    vmem = pl.BlockSpec(memory_space=pltpu.VMEM)
    away = pl.BlockSpec(memory_space=pltpu.HBM)
    operands = [by_longitude(fields).reshape(members, cells, channels), mix_weight, spectral_weight.transpose(1, 0, 2), mode_limit,
                jnp.asarray(forward), jnp.asarray(inverse)]
    in_specs = [away] * 6
    out_shape = [jax.ShapeDtypeStruct((members, cells, channels), jnp.bfloat16)]
    if fused:
        latitude = np.float32(-0.5 * math.pi) + (
            np.arange(nlat, dtype=np.float32) + np.float32(0.5)
        ) * np.float32(math.pi / nlat)
        cosines = np.zeros((nlat + 2, half), np.float32)
        cosines[1:-1] = np.cos(latitude)[:, None]
        operands += [by_longitude(forcing), land_mask, jnp.asarray(cosines)]
        in_specs += [away] * 3
        out_shape += [
            jax.ShapeDtypeStruct((members * cells, half), jnp.float32),
        ]
    gat_rows = -(-2 * per // 8) * 8
    dma = pltpu.SemaphoreType.DMA
    results = pl.pallas_call(
        functools.partial(
            layer_kernel, n, lat_dev, own, length, slope, polar, fused
        ),
        out_shape=out_shape,
        in_specs=in_specs,
        out_specs=[away] + [vmem] * (len(out_shape) - 1),
        scratch_shapes=[
            pltpu.VMEM((members, cells, channels), jnp.bfloat16),
            dma((members,)),
            pltpu.VMEM((members, cells, channels), jnp.bfloat16),
            pltpu.VMEM(mix_weight.shape, jnp.bfloat16),
            pltpu.VMEM((per, 2, channels), jnp.float32),
            pltpu.SMEM(mode_limit.shape, jnp.int32),
            pltpu.VMEM(land_mask.shape, jnp.int32),
            pltpu.VMEM((nlat + 2, half), jnp.float32),
            pltpu.VMEM((lat_dev, own, half), jnp.float32),
            pltpu.VMEM((rows, pad, channels), jnp.bfloat16),
            pltpu.VMEM((channels // 128, pad * lat_dev, 128), jnp.float32),
            pltpu.VMEM((rows, pad, channels), jnp.bfloat16),
            pltpu.VMEM((n, gat_rows, channels), jnp.float32),
            pltpu.VMEM((modes, channels), jnp.float32),
            pltpu.VMEM((modes, channels), jnp.float32),
            pltpu.VMEM((chunks, n * pad, channels), jnp.bfloat16),
            pltpu.VMEM((2 * modes, channels), jnp.bfloat16),
            pltpu.VMEM((rows, pad, channels), jnp.bfloat16),
            pltpu.VMEM(forward.shape, jnp.bfloat16),
            pltpu.VMEM(inverse.shape, jnp.bfloat16),
            pltpu.VMEM((members * cells, half) if fused else (8, half), jnp.float32),
            pltpu.VMEM((n, 8, half), jnp.float32),
            pltpu.VMEM((own, half), jnp.float32),
            dma((chunks,)), dma((chunks,)), dma, dma((rows,)), dma((2,)), dma((2,)),
            dma((members + 8,)), dma, dma,
        ],
        compiler_params=pltpu.CompilerParams(
            collective_id=0, has_side_effects=True, vmem_limit_bytes=62 * 2**20
        ),
    )(*operands)
    layer_out = by_latitude(results[0])
    if fused:
        residual = by_latitude(results[1])
        return layer_out, residual
    zonal = extended(layer_out[..., :half], "lon", 2).astype(jnp.float32)
    zonal = (zonal[:, :, 2:] - zonal[:, :, :-2]) * slope
    merid = extended(layer_out[..., half:], "lat", 1).astype(jnp.float32)
    lat_ids = lax.axis_index("lat") * lat_dev + jnp.arange(-1, lat_dev + 1, dtype=jnp.int32)
    latitude = -0.5 * math.pi + (lat_ids.astype(jnp.float32) + 0.5) * (math.pi / nlat)
    cos_lat = jnp.cos(latitude)
    weighted = merid * cos_lat[None, :, None, None]
    merid = (weighted[:, 2:] - weighted[:, :-2]) * polar
    ocean = land_mask.astype(jnp.float32)[None, :, :, None]
    raw = ocean * (zonal + merid + cos_lat[1:-1][None, :, None, None] * forcing)
    total = lax.psum(jnp.sum(raw * raw), ("lon", "lat"))
    norm = jnp.sqrt(total / (members * nlat * length * half) + 1e-06)
    return layer_out, raw / norm


def solution(mesh):
    placed = (
        P(None, "lat", "lon", None),
        P(),
        P(None, "lon", None),
        P("lat"),
        P("lat", "lon"),
        P(None, "lat", "lon", None),
    )
    return jax.shard_map(
        per_device,
        mesh=mesh,
        in_specs=placed,
        out_specs=(P(None, "lat", "lon", None), P(None, "lat", "lon", None)),
        check_vma=False,
    )
```
